512 devices in a mesh: tm: 8 (over z_hi, core), particle: 8 (over y), cell: 8 (over x, z_lo).
Axes of the slice: x: 4, y: 8, z: 8 (z_hi: 4, z_lo: 2; z = z_hi * 2 + z_lo), core: 2. Of those that a mesh axis runs over, the one named last changes fastest.
Arguments:
- particles: float32 [8, 30, 8192], P('tm', None, 'particle'), may hold values from -50 to 50
- cell_points: float32 [8, 30, 8192], P('tm', None, 'cell'), may hold values from -50 to 50
- cell_counts: int32 [8], replicated, may hold values from 1365 to 8192, as said below
- brownian: float32 [8, 30, 8192], P('tm', None, ('particle', 'cell')), may hold values from -6 to 6
Outputs:
- descent_direction: float32 [8, 30, 8192], P('tm', None, ('particle', 'cell'))
- updated_particles: float32 [8, 30, 8192], P('tm', None, ('particle', 'cell'))
The draws below stay inside these ranges and needn't reach their ends.
Inputs may be any that keep to these rules, and one draw needn't show every extreme that they name: `cell_counts`: some time has all 8192 cells observed.
All inputs are finite; a program needn't handle non-finite values.
Results may differ from the reference program's by a relative error of at most 0.0003.
Values sent between devices are 32-bit elements; how exact they have to be, the bound alone decides.
A program may use at most 64 MiB of HBM per device.

```python
import math
import jax
import jax.numpy as jnp
from jax import lax

DIMS = 30
TIMES = 8
PARTICLES = 8192
CELLS = 8192


def point_cloud(key, salt_value, point_total):
    base_key = jax.random.fold_in(key, salt_value)
    normal_key = jax.random.fold_in(base_key, 1)
    scale_key = jax.random.fold_in(base_key, 2)
    standard = jnp.clip(jax.random.normal(normal_key, (TIMES, DIMS, point_total), jnp.float32), -6.0, 6.0)
    scales = jnp.exp(jax.random.uniform(scale_key, (TIMES, 1, point_total), jnp.float32, 0.0, math.log(4.0)))
    return standard * scales


def draw_particles(key, part):
    return point_cloud(key, 11, PARTICLES)


def draw_cell_points(key, part):
    return point_cloud(key, 23, CELLS)


def draw_cell_counts(key, part):
    first_key = jax.random.fold_in(key, 31)
    second_key = jax.random.fold_in(key, 37)
    sampled = jax.random.randint(first_key, (TIMES,), CELLS // 6, CELLS + 1, dtype=jnp.int32)
    fullest = jax.random.randint(second_key, (), 0, TIMES, dtype=jnp.int32)
    return jnp.where(jnp.arange(TIMES, dtype=jnp.int32) == fullest, CELLS, sampled).astype(jnp.int32)


def block_levels(stream_key, extent, split, least, largest):
    level, own = 1.0, jax.random.fold_in(stream_key, 6)
    for axis_at, parts in split:
        heights = jnp.exp(jax.random.uniform(jax.random.fold_in(own, axis_at), (parts,), jnp.float32, least / len(split), largest / len(split)))
        level = level * jnp.repeat(heights, extent[axis_at] // parts).reshape([-1 if axis == axis_at else 1 for axis in range(len(extent))])
    return level


def centred(own_key, extent, deviation, bound, split=(), held_as=jnp.bfloat16):
    drawn = deviation * jax.random.normal(own_key, extent, jnp.float32)
    if split:
        drawn = drawn * block_levels(own_key, extent, split, -0.22, 0.18)
    return jnp.clip(drawn, -bound, bound).astype(held_as)


def setup_inputs(seed: int = 0) -> dict:
    splits = jax.random.split(jax.random.key(seed), 5)
    particles = draw_particles(jax.random.fold_in(splits[4], 71), 0)
    cell_points = draw_cell_points(jax.random.fold_in(splits[4], 71), 0)
    cell_counts = draw_cell_counts(jax.random.fold_in(splits[4], 71), 0)
    brownian = centred(splits[3], (TIMES, DIMS, PARTICLES), 1.0, 6.0, ((0, 8), (2, 64)), jnp.float32)
    return dict(particles=particles, cell_points=cell_points, cell_counts=cell_counts, brownian=brownian)


DATA_VAR = 2.0
BRIDGE_VAR = 1.5
LANGEVIN_STRIDE = 0.05
NOISE_LEVEL = 1.0

def soft_mean(queries, targets, usable, spread):
    highest = lax.Precision.HIGHEST
    cross_terms = jnp.dot(queries.T, targets, precision=highest, preferred_element_type=jnp.float32)
    scores = (2.0 * cross_terms - lax.optimization_barrier(jnp.sum(queries * queries, 0))[:, None] - lax.optimization_barrier(jnp.sum(targets * targets, 0))[None, :]) / (2.0 * spread)
    scores = jnp.where(usable[None, :], scores, -jnp.inf)
    weights = jax.nn.softmax(scores, axis=1)
    return jnp.dot(targets, weights.T, precision=highest, preferred_element_type=jnp.float32)

def blockwise(queries, targets, usable, spread):
    row_span = math.gcd(queries.shape[1], 512)
    row_pieces = queries.reshape(queries.shape[0], -1, row_span).transpose(1, 0, 2)
    block_means = lax.map(lambda row_piece: soft_mean(row_piece, targets, usable, spread), row_pieces)
    return block_means.transpose(1, 0, 2).reshape(queries.shape)

def reference(particles, cell_points, cell_counts, brownian):
    positions = jnp.arange(CELLS, dtype=jnp.int32)
    everyone = jnp.ones((PARTICLES,), dtype=bool)
    drift_list = []
    moved_list = []
    for time_increment in range(TIMES):
        present_positions = particles[time_increment]
        usable = positions < cell_counts[time_increment]
        fit_mean = blockwise(present_positions, cell_points[time_increment], usable, DATA_VAR)
        gradient = (present_positions - fit_mean) / DATA_VAR
        if time_increment > 0:
            prior_mean = blockwise(present_positions, particles[time_increment - 1], everyone, BRIDGE_VAR)
            gradient = gradient + (present_positions - prior_mean) / BRIDGE_VAR
        if time_increment < TIMES - 1:
            later_mean = blockwise(present_positions, particles[time_increment + 1], everyone, BRIDGE_VAR)
            gradient = gradient + (present_positions - later_mean) / BRIDGE_VAR
        descent_direction = -gradient
        updated_particles = present_positions + LANGEVIN_STRIDE * descent_direction + math.sqrt(2.0 * LANGEVIN_STRIDE * NOISE_LEVEL) * brownian[time_increment]
        drift_list.append(descent_direction)
        moved_list.append(updated_particles)
    return (jnp.stack(drift_list), jnp.stack(moved_list))
```

```python
import functools
import math

import jax
import jax.numpy as jnp
from jax import lax
from jax.experimental import pallas as pl
from jax.experimental.pallas import tpu as pltpu
from jax.sharding import PartitionSpec as P

DATA_VAR = 2.0
BRIDGE_VAR = 1.5
LANGEVIN_STRIDE = 0.05
NOISE_LEVEL = 1.0
MASKED_SCORE = -1e30
LOG2E = math.log2(math.e)
MESH = pl.DeviceIdType.MESH
bf16, f32 = jnp.bfloat16, jnp.float32
ROWS = 32
CHUNK = 512


def split3(x):
    high = x.astype(bf16)
    rest = x - high.astype(f32)
    low = rest.astype(bf16)
    return high, low, (rest - low.astype(f32)).astype(bf16)


def query_stack(q):
    count = q.shape[1]
    ext = jnp.concatenate([q, jnp.ones((1, count), f32), jnp.zeros((1, count), f32)], 0)
    h, l, ll = split3(ext)
    return jnp.concatenate([h, h, l, l, h, ll], 0)


def target_stack(t, alpha, usable=None):
    count = t.shape[1]
    bias = -alpha * jnp.sum(t * t, 0, keepdims=True)
    if usable is not None:
        bias = jnp.where(usable, bias, MASKED_SCORE)
    ext = jnp.concatenate([t * (2.0 * alpha), bias, jnp.zeros((1, count), f32)], 0)
    h, l, ll = split3(ext)
    stack = jnp.concatenate([h, l, h, l, ll, h], 0)
    row = lax.broadcasted_iota(jnp.int32, ext.shape, 0)
    wh = jnp.where(row == 30, 1.0, h.astype(f32)).astype(bf16)
    wl = jnp.where(row == 30, 0.0, l.astype(f32)).astype(bf16)
    return stack, wh, wl


def kernel(
    sizes,
    counts, x_hbm, cells_hbm, noise_hbm,
    d_out, u_out,
    x_ref, cells_ref, noise_ref, near, queries, targets, scores, parts, got,
    in_sem, near_send, near_recv, part_send, part_recv,
):
    times, peers = sizes
    t, p, c = (lax.axis_index(a) for a in ("tm", "particle", "cell"))
    block = x_ref.shape[1]
    share = block // peers

    loads = [
        pltpu.make_async_copy(x_hbm.at[0], x_ref, in_sem.at[0]),
        pltpu.make_async_copy(cells_hbm.at[0], cells_ref, in_sem.at[1]),
        pltpu.make_async_copy(noise_hbm.at[0], noise_ref, in_sem.at[2]),
    ]
    for load in loads:
        load.start()

    after, before = lax.rem(t + 1, times), lax.rem(t + times - 1, times)
    others = [(after, c, p), (before, c, p)]
    mates = [(t, p, lax.rem(c + k, peers)) for k in range(1, peers)]
    barrier = pltpu.get_barrier_semaphore()
    for device in others + mates:
        pl.semaphore_signal(barrier, inc=1, device_id=device, device_id_type=MESH)
    pl.semaphore_wait(barrier, len(others) + len(mates))

    moves = [
        pltpu.make_async_remote_copy(
            src_ref=x_hbm.at[0], dst_ref=near.at[i],
            send_sem=near_send.at[i], recv_sem=near_recv.at[i],
            device_id=device, device_id_type=MESH,
        )
        for i, device in enumerate(others)
    ]
    for move in moves:
        move.start()

    loads[0].wait()
    queries[...] = query_stack(x_ref[...])

    def tile(which, raw, alpha, usable=None):
        stack, wh, wl = target_stack(raw, alpha, usable)
        targets[...] = stack.T
        both = jnp.concatenate([wh, wl], 0)

        def score(i):
            s = jnp.dot(
                targets[...], queries[:, i * CHUNK:(i + 1) * CHUNK], preferred_element_type=f32
            )
            scores[i % 2] = s
            return jnp.max(s, 0, keepdims=True)

        rounds = block // CHUNK
        top = score(0)
        for i in range(rounds):
            next_top = score(i + 1) if i + 1 < rounds else None
            e = jnp.exp2(scores[i % 2] - top)
            eh = e.astype(bf16)
            el = (e - eh.astype(f32)).astype(bf16)
            o = jnp.dot(both, eh, preferred_element_type=f32)
            o = o[:ROWS] + o[ROWS:] + jnp.dot(wh, el, preferred_element_type=f32)
            row = lax.broadcasted_iota(jnp.int32, o.shape, 0)
            o = jnp.where(row == ROWS - 1, top, o)
            for j in range(CHUNK // share):
                parts[which, i * (CHUNK // share) + j] = o[:, j * share:(j + 1) * share]
            top = next_top

        sends = []
        for k in range(1, peers):
            send = pltpu.make_async_remote_copy(
                src_ref=parts.at[which, lax.rem(c + k, peers)], dst_ref=got.at[which, k - 1],
                send_sem=part_send.at[which, k - 1], recv_sem=part_recv.at[which, k - 1],
                device_id=mates[k - 1], device_id_type=MESH,
            )
            send.start()
            sends.append(send)
        return sends

    def mean(which, sends, alpha):
        pieces = [parts[which, c]]
        for k, send in enumerate(sends):
            send.wait_recv()
            pieces.append(got[which, k])
        top = functools.reduce(jnp.maximum, [x[ROWS - 1:] for x in pieces])
        total = functools.reduce(jnp.add, [x * jnp.exp2(x[ROWS - 1:] - top) for x in pieces])
        return total[:30] / (total[30:31] * (2.0 * alpha))

    fit_alpha, bridge_alpha = (LOG2E / (2.0 * v) for v in (DATA_VAR, BRIDGE_VAR))
    loads[1].wait()
    cell = c * cells_ref.shape[1] + lax.broadcasted_iota(jnp.int32, (1, cells_ref.shape[1]), 1)
    sends = [tile(0, cells_ref[...], fit_alpha, cell < counts[t])]
    for i in (0, 1):
        moves[i].wait_recv()
        sends.append(tile(1 + i, near[i], bridge_alpha))
    loads[2].wait()
    means = [mean(i, sends[i], (fit_alpha, bridge_alpha, bridge_alpha)[i]) for i in range(3)]

    own = x_ref[:, pl.ds(pl.multiple_of(c * share, share), share)]
    has_prior = (t > 0).astype(f32)
    has_later = (t < times - 1).astype(f32)
    gradient = (own - means[0]) / DATA_VAR
    gradient = gradient + has_prior * (own - means[1]) / BRIDGE_VAR
    gradient = gradient + has_later * (own - means[2]) / BRIDGE_VAR
    d_out[0] = -gradient
    u_out[0] = (
        own - LANGEVIN_STRIDE * gradient
        + math.sqrt(2.0 * LANGEVIN_STRIDE * NOISE_LEVEL) * noise_ref[...]
    )
    for move in moves:
        move.wait_send()
    for group in sends:
        for send in group:
            send.wait_send()


def shards(sizes, particles, cell_points, cell_counts, brownian):
    _, dims, block = particles.shape
    cells = cell_points.shape[2]
    share = brownian.shape[2]
    peers = sizes[1]
    any_spec = pl.BlockSpec(memory_space=pl.ANY)
    vmem = pl.BlockSpec(memory_space=pltpu.VMEM)
    dma = pltpu.SemaphoreType.DMA
    return pl.pallas_call(
        functools.partial(kernel, sizes),
        out_shape=[jax.ShapeDtypeStruct((1, dims, share), f32)] * 2,
        in_specs=[pl.BlockSpec(memory_space=pltpu.SMEM), any_spec, any_spec, any_spec],
        out_specs=[vmem, vmem],
        scratch_shapes=[
            pltpu.VMEM((dims, block), f32),
            pltpu.VMEM((dims, cells), f32),
            pltpu.VMEM((dims, share), f32),
            pltpu.VMEM((2, dims, block), f32),
            pltpu.VMEM((6 * ROWS, block), bf16),
            pltpu.VMEM((max(block, cells), 6 * ROWS), bf16),
            pltpu.VMEM((2, max(block, cells), CHUNK), f32),
            pltpu.VMEM((3, peers, ROWS, share), f32),
            pltpu.VMEM((3, peers - 1, ROWS, share), f32),
            dma((3,)), dma((2,)), dma((2,)), dma((3, peers - 1)), dma((3, peers - 1)),
        ],
        compiler_params=pltpu.CompilerParams(
            collective_id=0, has_side_effects=True, vmem_limit_bytes=40 * 2**20
        ),
        name="langevin",
    )(cell_counts, particles, cell_points, brownian)


def solution(mesh):
    in_specs = (
        P("tm", None, "particle"),
        P("tm", None, "cell"),
        P(),
        P("tm", None, ("particle", "cell")),
    )
    out_specs = (P("tm", None, ("particle", "cell")), P("tm", None, ("particle", "cell")))
    sizes = (mesh.shape["tm"], mesh.shape["cell"])
    return jax.shard_map(
        functools.partial(shards, sizes),
        mesh=mesh, in_specs=in_specs, out_specs=out_specs, check_vma=False,
    )
```

```python
import functools
import math

import jax
import jax.numpy as jnp
from jax import lax
from jax.experimental import pallas as pl
from jax.experimental.pallas import tpu as pltpu
from jax.sharding import PartitionSpec as P

DATA_VAR = 2.0
BRIDGE_VAR = 1.5
LANGEVIN_STRIDE = 0.05
NOISE_LEVEL = 1.0
MASKED_SCORE = -1e30
LOG2E = math.log2(math.e)
MESH = pl.DeviceIdType.MESH
bf16, f32 = jnp.bfloat16, jnp.float32
ROWS = 32
CHUNK = 512


def split3(x):
    high = x.astype(bf16)
    rest = x - high.astype(f32)
    low = rest.astype(bf16)
    return high, low, (rest - low.astype(f32)).astype(bf16)


def query_stack(q):
    count = q.shape[1]
    ext = jnp.concatenate([q, jnp.ones((1, count), f32), jnp.zeros((1, count), f32)], 0)
    h, l, ll = split3(ext)
    return jnp.concatenate([h, h, l, l, h, ll], 0)


def target_stack(t, alpha, usable=None):
    count = t.shape[1]
    bias = -alpha * jnp.sum(t * t, 0, keepdims=True)
    if usable is not None:
        bias = jnp.where(usable, bias, MASKED_SCORE)
    ext = jnp.concatenate([t * (2.0 * alpha), bias, jnp.zeros((1, count), f32)], 0)
    h, l, ll = split3(ext)
    stack = jnp.concatenate([h, l, h, l, ll, h], 0)
    row = lax.broadcasted_iota(jnp.int32, ext.shape, 0)
    wh = jnp.where(row == 30, 1.0, h.astype(f32)).astype(bf16)
    wl = jnp.where(row == 30, 0.0, l.astype(f32)).astype(bf16)
    return stack.T, jnp.concatenate([wh, wl], 0)


def kernel(
    sizes,
    counts_hbm, x_hbm, cells_hbm, noise_hbm,
    d_out, u_out,
    counts, x_ref, cells_ref, noise_ref, near, slices, queries, targets, weights, scores, parts, got, done,
    in_sem, near_send, near_recv, slice_send, slice_recv, part_send, part_recv,
):
    times, blocks, peers = sizes
    t, p, c = (lax.axis_index(a) for a in ("tm", "particle", "cell"))
    share = noise_ref.shape[1]
    order = sorted(range(blocks), key=lambda k: -min(k, blocks - k))
    mine = pl.ds(pl.multiple_of(c * share, share), share)

    def local(src, dst, sem):
        copy = pltpu.make_async_copy(src, dst, sem)
        copy.start()
        return copy

    def remote(src, dst, send, recv, device):
        copy = pltpu.make_async_remote_copy(
            src_ref=src, dst_ref=dst, send_sem=send, recv_sem=recv,
            device_id=device, device_id_type=MESH,
        )
        copy.start()
        return copy

    load_x = local(x_hbm.at[:, 0, :], x_ref, in_sem.at[0])
    load_cells = local(cells_hbm.at[:, 0, :], cells_ref, in_sem.at[1])
    load_noise = local(noise_hbm.at[:, 0, :], noise_ref, in_sem.at[2])
    load_counts = local(counts_hbm, counts, in_sem.at[3])

    after, before = lax.rem(t + 1, times), lax.rem(t + times - 1, times)
    times_near = [(after, p, c), (before, p, c)]
    row_to = {k: (t, lax.rem(p + k, blocks), c) for k in range(1, blocks)}
    cell_to = {k: (t, p, lax.rem(c + k, peers)) for k in range(1, peers)}
    greeted = [row_to[k] for k in order if k] + times_near + list(cell_to.values())
    barrier = pltpu.get_barrier_semaphore()
    for device in greeted:
        pl.semaphore_signal(barrier, inc=1, device_id=device, device_id_type=MESH)
    pl.semaphore_wait(barrier, len(greeted))

    moves = [
        remote(x_hbm.at[:, 0, mine], slices.at[i], slice_send.at[i], slice_recv.at[i], row_to[k])
        for i, k in enumerate(order) if k
    ]
    moves += [
        remote(x_hbm.at[:, 0, :], near.at[i], near_send.at[i], near_recv.at[i], device)
        for i, device in enumerate(times_near)
    ]

    def score(which, queries_at, half, slot):
        s = jnp.dot(
            targets[which], queries[queries_at, :, half * CHUNK:(half + 1) * CHUNK],
            preferred_element_type=f32,
        )
        scores[slot] = s
        return jnp.max(s, 0, keepdims=True)

    def weigh(which, slot, top):
        e = jnp.exp2(scores[slot] - top)
        eh = e.astype(bf16)
        el = (e - eh.astype(f32)).astype(bf16)
        o = jnp.dot(weights[which], eh, preferred_element_type=f32)
        o = o[:ROWS] + o[ROWS:]
        o = o + jnp.dot(weights[which, :ROWS], el, preferred_element_type=f32)
        row = lax.broadcasted_iota(jnp.int32, o.shape, 0)
        return jnp.where(row == ROWS - 1, top, o)

    def prepare(which, raw, alpha, usable=None):
        targets[which], weights[which] = target_stack(raw, alpha, usable)

    fit_alpha, bridge_alpha = (LOG2E / (2.0 * v) for v in (DATA_VAR, BRIDGE_VAR))
    per = CHUNK // share
    halves = blocks // per

    def work(steps, after_step):
        top = score(*steps[0], 0)
        for i, step in enumerate(steps):
            next_top = score(*steps[i + 1], (i + 1) % 2) if i + 1 < len(steps) else None
            which, _, half = step
            o = weigh(which, i % 2, top)
            for j in range(per):
                parts[which, half * per + j] = o[:, j * share:(j + 1) * share]
            after_step(which, half)
            top = next_top

    load_x.wait()
    queries[0] = query_stack(x_ref[...])
    load_cells.wait()
    load_counts.wait()
    cell = c * cells_ref.shape[1] + lax.broadcasted_iota(jnp.int32, (1, cells_ref.shape[1]), 1)
    prepare(0, cells_ref[...], fit_alpha, cell < counts[t])
    work([(0, 0, half) for half in range(halves)], lambda which, half: None)
    sends = {}
    for k in range(1, peers):
        sends[0, k] = remote(
            parts.at[0, lax.rem(c + k, peers)], got.at[0, k],
            part_send.at[0, k], part_recv.at[0, k], cell_to[k],
        )

    own = x_ref[:, mine]
    for i, k in enumerate(order):
        if k:
            moves[i].wait_recv()
            queries[1, :, i * share:(i + 1) * share] = query_stack(slices[i])
        else:
            queries[1, :, i * share:(i + 1) * share] = query_stack(own)
    for i in (0, 1):
        moves[blocks - 1 + i].wait_recv()
        prepare(1 + i, near[i], bridge_alpha)

    def hand_back(which, half):
        for i in range(half * per, (half + 1) * per):
            if order[i]:
                sends[which, i] = remote(
                    parts.at[which, i], got.at[which, i],
                    part_send.at[which, i], part_recv.at[which, i], row_to[blocks - order[i]],
                )

    work([(which, 1, half) for half in range(halves) for which in (1, 2)], hand_back)

    def mean(which, home, alpha):
        pieces = [parts[which, home]]
        for (kind, i), send in sends.items():
            if kind == which:
                send.wait_recv()
                pieces.append(got[which, i])
        top = functools.reduce(jnp.maximum, [x[ROWS - 1:] for x in pieces])
        total = functools.reduce(jnp.add, [x * jnp.exp2(x[ROWS - 1:] - top) for x in pieces])
        return total[:30] / (total[30:31] * (2.0 * alpha))

    fit_mean = mean(0, c, fit_alpha)
    prior_mean = mean(1, blocks - 1, bridge_alpha)
    later_mean = mean(2, blocks - 1, bridge_alpha)
    has_prior = (t > 0).astype(f32)
    has_later = (t < times - 1).astype(f32)
    gradient = (own - fit_mean) / DATA_VAR
    gradient = gradient + has_prior * (own - prior_mean) / BRIDGE_VAR
    gradient = gradient + has_later * (own - later_mean) / BRIDGE_VAR
    load_noise.wait()
    done[0] = -gradient
    stores = [local(done.at[0], d_out.at[:, 0, :], in_sem.at[0])]
    done[1] = (
        own - LANGEVIN_STRIDE * gradient
        + math.sqrt(2.0 * LANGEVIN_STRIDE * NOISE_LEVEL) * noise_ref[...]
    )
    stores.append(local(done.at[1], u_out.at[:, 0, :], in_sem.at[1]))
    for copy in stores:
        copy.wait()
    for copy in moves + list(sends.values()):
        copy.wait_send()


def shards(sizes, particles, cell_points, cell_counts, brownian):
    _, dims, block = particles.shape
    cells = cell_points.shape[2]
    share = brownian.shape[2]
    _, blocks, peers = sizes
    assert blocks * share == block == cells and peers == blocks
    any_spec = pl.BlockSpec(memory_space=pl.ANY)
    dma = pltpu.SemaphoreType.DMA
    outs = pl.pallas_call(
        functools.partial(kernel, sizes),
        out_shape=[jax.ShapeDtypeStruct((dims, 1, share), f32)] * 2,
        in_specs=[any_spec] * 4,
        out_specs=[any_spec] * 2,
        scratch_shapes=[
            pltpu.SMEM(cell_counts.shape, jnp.int32),
            pltpu.VMEM((dims, block), f32),
            pltpu.VMEM((dims, cells), f32),
            pltpu.VMEM((dims, share), f32),
            pltpu.VMEM((2, dims, block), f32),
            pltpu.VMEM((blocks, dims, share), f32),
            pltpu.VMEM((2, 6 * ROWS, block), bf16),
            pltpu.VMEM((3, block, 6 * ROWS), bf16),
            pltpu.VMEM((3, 2 * ROWS, block), bf16),
            pltpu.VMEM((2, block, CHUNK), f32),
            pltpu.VMEM((3, blocks, ROWS, share), f32),
            pltpu.VMEM((3, blocks, ROWS, share), f32),
            pltpu.VMEM((2, dims, share), f32),
            dma((4,)), dma((2,)), dma((2,)), dma((blocks,)), dma((blocks,)),
            dma((3, blocks)), dma((3, blocks)),
        ],
        compiler_params=pltpu.CompilerParams(
            collective_id=0, has_side_effects=True, vmem_limit_bytes=62 * 2**20
        ),
        name="langevin",
    )(cell_counts, *(a.transpose(1, 0, 2) for a in (particles, cell_points, brownian)))
    return tuple(o.transpose(1, 0, 2) for o in outs)


def solution(mesh):
    in_specs = (
        P("tm", None, "particle"),
        P("tm", None, "cell"),
        P(),
        P("tm", None, ("particle", "cell")),
    )
    out_specs = (P("tm", None, ("particle", "cell")), P("tm", None, ("particle", "cell")))
    sizes = tuple(mesh.shape[a] for a in ("tm", "particle", "cell"))
    return jax.shard_map(
        functools.partial(shards, sizes),
        mesh=mesh, in_specs=in_specs, out_specs=out_specs, check_vma=False,
    )
```

```python
import functools
import math

import jax
import jax.numpy as jnp
from jax import lax
from jax.experimental import pallas as pl
from jax.experimental.pallas import tpu as pltpu
from jax.sharding import PartitionSpec as P

DATA_VAR = 2.0
BRIDGE_VAR = 1.5
LANGEVIN_STRIDE = 0.05
NOISE_LEVEL = 1.0
MASKED_SCORE = -1e30
LOG2E = math.log2(math.e)
MESH = pl.DeviceIdType.MESH
bf16, f32 = jnp.bfloat16, jnp.float32
ROWS = 32
CHUNK = 512


def split3(x):
    high = x.astype(bf16)
    rest = x - high.astype(f32)
    low = rest.astype(bf16)
    return high, low, (rest - low.astype(f32)).astype(bf16)


def query_stack(q):
    count = q.shape[1]
    ext = jnp.concatenate([q, jnp.ones((1, count), f32), jnp.zeros((1, count), f32)], 0)
    h, l, ll = split3(ext)
    return jnp.concatenate([h, h, l, l, h, ll], 0)


def target_stack(t, alpha, usable=None):
    count = t.shape[1]
    bias = -alpha * jnp.sum(t * t, 0, keepdims=True)
    if usable is not None:
        bias = jnp.where(usable, bias, MASKED_SCORE)
    ext = jnp.concatenate([t * (2.0 * alpha), bias, jnp.zeros((1, count), f32)], 0)
    h, l, ll = split3(ext)
    stack = jnp.concatenate([h, l, h, l, ll, h], 0)
    row = lax.broadcasted_iota(jnp.int32, ext.shape, 0)
    wh = jnp.where(row == 30, 1.0, h.astype(f32)).astype(bf16)
    wl = jnp.where(row == 30, 0.0, l.astype(f32)).astype(bf16)
    return stack.T, jnp.concatenate([wh, wl], 0)


def kernel(
    sizes,
    counts_hbm, x_hbm, cells_hbm, noise_hbm,
    g_out, moved_out,
    counts, x_ref, cells_ref, noise_ref, near, slices, queries, targets, weights, scores, parts, got, twin_sums, pair_sums,
    in_sem, near_send, near_recv, slice_send, slice_recv, part_send, part_recv, twin_sem,
):
    times, blocks, peers = sizes
    t, p, c = (lax.axis_index(a) for a in ("tm", "particle", "cell"))
    share = noise_ref.shape[1]
    order = sorted(range(blocks), key=lambda k: -min(k, blocks - k))
    mine = pl.ds(pl.multiple_of(c * share, share), share)

    def local(src, dst, sem):
        copy = pltpu.make_async_copy(src, dst, sem)
        copy.start()
        return copy

    def remote(src, dst, send, recv, device, start=True):
        copy = pltpu.make_async_remote_copy(
            src_ref=src, dst_ref=dst, send_sem=send, recv_sem=recv,
            device_id=device, device_id_type=MESH,
        )
        if start:
            copy.start()
        return copy

    load_x = local(x_hbm.at[:, 0, :], x_ref, in_sem.at[0])
    load_cells = local(cells_hbm.at[:, 0, :], cells_ref, in_sem.at[1])
    load_noise = local(noise_hbm.at[:, 0, :], noise_ref, in_sem.at[2])
    load_counts = local(counts_hbm, counts, in_sem.at[3])

    after, before = lax.rem(t + 1, times), lax.rem(t + times - 1, times)
    times_near = [(after, p, c), (before, p, c)]
    has_prior, has_later = t > 0, t < times - 1
    goes, comes = (has_later, has_prior), (has_prior, has_later)
    row_to = {k: (t, lax.rem(p + k, blocks), c) for k in range(1, blocks)}
    pairs = peers // 2
    x, side = lax.div(c, 2), lax.rem(c, 2)
    twin = (t, p, 2 * x + 1 - side)
    pair_to = {k: (t, p, 2 * lax.rem(x + k, pairs) + side) for k in range(1, pairs)}
    greeted = [row_to[k] for k in order if k] + [twin] + list(pair_to.values())
    barrier = pltpu.get_barrier_semaphore()

    def greet(device):
        pl.semaphore_signal(barrier, inc=1, device_id=device, device_id_type=MESH)

    for device in greeted:
        greet(device)
    for go, device in zip(goes, times_near):
        pl.when(go)(functools.partial(greet, device))
    pl.semaphore_wait(
        barrier, len(greeted) + has_prior.astype(jnp.int32) + has_later.astype(jnp.int32)
    )

    blocks_in = [
        remote(x_hbm.at[:, 0, :], near.at[i], near_send.at[i], near_recv.at[i], device, False)
        for i, device in enumerate(times_near)
    ]
    for go, copy in zip(goes, blocks_in):
        pl.when(go)(copy.start)
    slices_in = [
        remote(x_hbm.at[:, 0, mine], slices.at[i], slice_send.at[i], slice_recv.at[i], row_to[k])
        for i, k in enumerate(order) if k
    ]

    def score(which, queries_at, half, slot):
        s = jnp.dot(
            targets[which], queries[queries_at, :, half * CHUNK:(half + 1) * CHUNK],
            preferred_element_type=f32,
        )
        scores[slot] = s
        return jnp.max(s, 0, keepdims=True)

    def weigh(which, slot, top):
        e = jnp.exp2(scores[slot] - top)
        eh = e.astype(bf16)
        el = (e - eh.astype(f32)).astype(bf16)
        o = jnp.dot(weights[which], eh, preferred_element_type=f32)
        o = o[:ROWS] + o[ROWS:]
        o = o + jnp.dot(weights[which, :ROWS], el, preferred_element_type=f32)
        row = lax.broadcasted_iota(jnp.int32, o.shape, 0)
        return jnp.where(row == ROWS - 1, top, o)

    def prepare(which, raw, alpha, usable=None):
        targets[which], weights[which] = target_stack(raw, alpha, usable)

    fit_alpha, bridge_alpha = (LOG2E / (2.0 * v) for v in (DATA_VAR, BRIDGE_VAR))
    per = CHUNK // share
    halves = blocks // per

    def work(steps, after_step):
        top = score(*steps[0], 0)
        for i, step in enumerate(steps):
            next_top = score(*steps[i + 1], (i + 1) % 2) if i + 1 < len(steps) else None
            which, _, half = step
            o = weigh(which, i % 2, top)
            for j in range(per):
                at = half * per + j
                if which == 0:
                    at = at % 2 * pairs + at // 2
                parts[which, at] = o[:, j * share:(j + 1) * share]
            after_step(which, half)
            top = next_top

    load_x.wait()
    queries[0] = query_stack(x_ref[...])
    load_cells.wait()
    load_counts.wait()
    cell = c * cells_ref.shape[1] + lax.broadcasted_iota(jnp.int32, (1, cells_ref.shape[1]), 1)
    prepare(0, cells_ref[...], fit_alpha, cell < counts[t])
    work([(0, 0, half) for half in range(halves)], lambda which, half: None)
    sends = {}
    to_twin = remote(
        parts.at[0, pl.ds((1 - side) * pairs, pairs)], twin_sums,
        twin_sem.at[0], twin_sem.at[1], twin,
    )

    def merge(pieces):
        top = functools.reduce(jnp.maximum, [q[ROWS - 1:] for q in pieces])
        total = functools.reduce(jnp.add, [q * jnp.exp2(q[ROWS - 1:] - top) for q in pieces])
        return top, total

    def share_fit():
        to_twin.wait_recv()
        for j in range(pairs):
            top, total = merge([parts[0, side * pairs + j], twin_sums[j]])
            row = lax.broadcasted_iota(jnp.int32, total.shape, 0)
            pair_sums[j] = jnp.where(row == ROWS - 1, top, total)
        for k in range(1, pairs):
            sends[0, k] = remote(
                pair_sums.at[lax.rem(x + k, pairs)], got.at[0, k],
                part_send.at[0, k], part_recv.at[0, k], pair_to[k],
            )

    own = x_ref[:, mine]
    queries[1, :, (blocks - 1) * share:] = query_stack(own)
    for i in (0, 1):
        pl.when(comes[i])(blocks_in[i].wait_recv)

        @pl.when(jnp.logical_not(comes[i]))
        def _():
            near[i] = jnp.zeros(near.shape[1:], f32)

        prepare(1 + i, near[i], bridge_alpha)
    for i, copy in enumerate(slices_in):
        copy.wait_recv()
        queries[1, :, i * share:(i + 1) * share] = query_stack(slices[i])

    def hand_back(which, half):
        if (which, half) == (2, 0):
            share_fit()
        for i in range(half * per, (half + 1) * per):
            if order[i]:
                sends[which, i] = remote(
                    parts.at[which, i], got.at[which, i],
                    part_send.at[which, i], part_recv.at[which, i], row_to[blocks - order[i]],
                    False,
                )

        @pl.when(comes[which - 1])
        def _():
            for i in range(half * per, (half + 1) * per):
                if order[i]:
                    sends[which, i].start()

    work([(which, 1, half) for half in range(halves) for which in (1, 2)], hand_back)

    def mean(which, home, alpha):
        pieces = [home] + [got[which, i] for kind, i in sends if kind == which]
        _, total = merge(pieces)
        return total[:30] / (total[30:31] * (2.0 * alpha))

    def settle(which, wait):
        for (kind, _), send in sends.items():
            if kind == which:
                wait(send)

    for wait in (lambda send: send.wait_recv(), lambda send: send.wait_send()):
        settle(0, wait)
        for i in (0, 1):
            pl.when(comes[i])(functools.partial(settle, 1 + i, wait))
    for go, copy in zip(goes, blocks_in):
        pl.when(go)(copy.wait_send)
    for copy in slices_in + [to_twin]:
        copy.wait_send()

    fit_mean = mean(0, pair_sums[x], fit_alpha)
    prior_mean = mean(1, parts[1, blocks - 1], bridge_alpha)
    later_mean = mean(2, parts[2, blocks - 1], bridge_alpha)
    gradient = (own - fit_mean) / DATA_VAR
    gradient = gradient + jnp.where(has_prior, (own - prior_mean) / BRIDGE_VAR, 0.0)
    gradient = gradient + jnp.where(has_later, (own - later_mean) / BRIDGE_VAR, 0.0)
    load_noise.wait()
    g_out[:, 0, :] = gradient
    moved_out[:, 0, :] = (
        own + math.sqrt(2.0 * LANGEVIN_STRIDE * NOISE_LEVEL) * noise_ref[...]
    )


def shards(sizes, particles, cell_points, cell_counts, brownian):
    _, dims, block = particles.shape
    cells = cell_points.shape[2]
    share = brownian.shape[2]
    _, blocks, peers = sizes
    assert blocks * share == block == cells and peers == blocks
    any_spec = pl.BlockSpec(memory_space=pl.ANY)
    dma = pltpu.SemaphoreType.DMA
    gradient, moved = pl.pallas_call(
        functools.partial(kernel, sizes),
        out_shape=[jax.ShapeDtypeStruct((dims, 1, share), f32)] * 2,
        in_specs=[any_spec] * 4,
        out_specs=[pl.BlockSpec(memory_space=pltpu.VMEM)] * 2,
        scratch_shapes=[
            pltpu.SMEM(cell_counts.shape, jnp.int32),
            pltpu.VMEM((dims, block), f32),
            pltpu.VMEM((dims, cells), f32),
            pltpu.VMEM((dims, share), f32),
            pltpu.VMEM((2, dims, block), f32),
            pltpu.VMEM((blocks, dims, share), f32),
            pltpu.VMEM((2, 6 * ROWS, block), bf16),
            pltpu.VMEM((3, block, 6 * ROWS), bf16),
            pltpu.VMEM((3, 2 * ROWS, block), bf16),
            pltpu.VMEM((2, block, CHUNK), f32),
            pltpu.VMEM((3, blocks, ROWS, share), f32),
            pltpu.VMEM((3, blocks, ROWS, share), f32),
            pltpu.VMEM((peers // 2, ROWS, share), f32),
            pltpu.VMEM((peers // 2, ROWS, share), f32),
            dma((4,)), dma((2,)), dma((2,)), dma((blocks,)), dma((blocks,)),
            dma((3, blocks)), dma((3, blocks)), dma((2,)),
        ],
        compiler_params=pltpu.CompilerParams(
            collective_id=0, has_side_effects=True, vmem_limit_bytes=2**26 - 64 * 2**10
        ),
        name="langevin",
    )(cell_counts, *(a.transpose(1, 0, 2) for a in (particles, cell_points, brownian)))
    gradient, moved = (a.transpose(1, 0, 2) for a in (gradient, moved))
    return -gradient, moved - LANGEVIN_STRIDE * gradient


def solution(mesh):
    in_specs = (
        P("tm", None, "particle"),
        P("tm", None, "cell"),
        P(),
        P("tm", None, ("particle", "cell")),
    )
    out_specs = (P("tm", None, ("particle", "cell")), P("tm", None, ("particle", "cell")))
    sizes = tuple(mesh.shape[a] for a in ("tm", "particle", "cell"))
    return jax.shard_map(
        functools.partial(shards, sizes),
        mesh=mesh, in_specs=in_specs, out_specs=out_specs, check_vma=False,
    )
```

```python
import functools
import math

import jax
import jax.numpy as jnp
from jax import lax
from jax.experimental import pallas as pl
from jax.experimental.pallas import tpu as pltpu
from jax.sharding import PartitionSpec as P

DATA_VAR = 2.0
BRIDGE_VAR = 1.5
LANGEVIN_STRIDE = 0.05
NOISE_LEVEL = 1.0
MASKED_SCORE = -1e30
LOG2E = math.log2(math.e)
MESH = pl.DeviceIdType.MESH
bf16, f32 = jnp.bfloat16, jnp.float32
ROWS = 32
CHUNK = 256


def split3(x):
    high = x.astype(bf16)
    rest = x - high.astype(f32)
    low = rest.astype(bf16)
    return high, low, (rest - low.astype(f32)).astype(bf16)


def query_stack(q):
    count = q.shape[1]
    ext = jnp.concatenate([q, jnp.ones((1, count), f32), jnp.zeros((1, count), f32)], 0)
    h, l, ll = split3(ext)
    return jnp.concatenate([h, h, l, l, h, ll], 0)


def target_stack(t, alpha, usable=None):
    count = t.shape[1]
    bias = -alpha * jnp.sum(t * t, 0, keepdims=True)
    if usable is not None:
        bias = jnp.where(usable, bias, MASKED_SCORE)
    ext = jnp.concatenate([t * (2.0 * alpha), bias, jnp.zeros((1, count), f32)], 0)
    h, l, ll = split3(ext)
    stack = jnp.concatenate([h, l, h, l, ll, h], 0)
    row = lax.broadcasted_iota(jnp.int32, ext.shape, 0)
    wh = jnp.where(row == 30, 1.0, h.astype(f32)).astype(bf16)
    wl = jnp.where(row == 30, 0.0, l.astype(f32)).astype(bf16)
    return stack.T, jnp.concatenate([wh, wl], 0)


def kernel(
    sizes,
    counts_hbm, x_hbm, cells_hbm, noise_hbm,
    g_out, moved_out,
    counts, x_ref, cells_ref, noise_ref, near, slices, queries, targets, weights, scores, parts, got, twin_sums, pair_sums,
    in_sem, near_send, near_recv, slice_send, slice_recv, part_send, part_recv, twin_sem,
):
    times, blocks, peers = sizes
    t, p, c = (lax.axis_index(a) for a in ("tm", "particle", "cell"))
    share = noise_ref.shape[1]
    order = sorted(range(blocks), key=lambda k: -min(k, blocks - k))
    mine = pl.ds(pl.multiple_of(c * share, share), share)

    def local(src, dst, sem):
        copy = pltpu.make_async_copy(src, dst, sem)
        copy.start()
        return copy

    def remote(src, dst, send, recv, device, start=True):
        copy = pltpu.make_async_remote_copy(
            src_ref=src, dst_ref=dst, send_sem=send, recv_sem=recv,
            device_id=device, device_id_type=MESH,
        )
        if start:
            copy.start()
        return copy

    after, before = lax.rem(t + 1, times), lax.rem(t + times - 1, times)
    times_near = [(after, p, c), (before, p, c)]
    has_prior, has_later = t > 0, t < times - 1
    goes, comes = (has_later, has_prior), (has_prior, has_later)
    row_to = {k: (t, lax.rem(p + k, blocks), c) for k in range(1, blocks)}
    pairs = peers // 2
    x, side = lax.div(c, 2), lax.rem(c, 2)
    twin = (t, p, 2 * x + 1 - side)
    pair_to = {k: (t, p, 2 * lax.rem(x + k, pairs) + side) for k in range(1, pairs)}
    greeted = [row_to[k] for k in order if k] + [twin] + list(pair_to.values())
    barrier = pltpu.get_barrier_semaphore()

    def greet(device):
        pl.semaphore_signal(barrier, inc=1, device_id=device, device_id_type=MESH)

    for device in greeted:
        greet(device)
    for go, device in zip(goes, times_near):
        pl.when(go)(functools.partial(greet, device))
    load_x = local(x_hbm.at[:, 0, :], x_ref, in_sem.at[0])
    load_cells = local(cells_hbm.at[:, 0, :], cells_ref, in_sem.at[1])
    load_noise = local(noise_hbm.at[:, 0, :], noise_ref, in_sem.at[2])
    load_counts = local(counts_hbm, counts, in_sem.at[3])
    pl.semaphore_wait(
        barrier, len(greeted) + has_prior.astype(jnp.int32) + has_later.astype(jnp.int32)
    )

    blocks_in = [
        remote(x_hbm.at[:, 0, :], near.at[i], near_send.at[i], near_recv.at[i], device, False)
        for i, device in enumerate(times_near)
    ]
    for go, copy in zip(goes, blocks_in):
        pl.when(go)(copy.start)
    slices_in = [
        remote(x_hbm.at[:, 0, mine], slices.at[i], slice_send.at[i], slice_recv.at[i], row_to[k])
        for i, k in enumerate(order) if k
    ]

    def score(which, queries_at, half, slot):
        if which:
            ready(which, half)
        s = jnp.dot(
            targets[which], queries[queries_at, :, half * CHUNK:(half + 1) * CHUNK],
            preferred_element_type=f32,
        )
        scores[slot] = s
        return jnp.max(s, 0, keepdims=True)

    def weigh(which, slot, top):
        e = jnp.exp2(scores[slot] - top)
        eh = e.astype(bf16)
        el = (e - eh.astype(f32)).astype(bf16)
        o = jnp.dot(weights[which], eh, preferred_element_type=f32)
        o = o[:ROWS] + o[ROWS:]
        o = o + jnp.dot(weights[which, :ROWS], el, preferred_element_type=f32)
        row = lax.broadcasted_iota(jnp.int32, o.shape, 0)
        return jnp.where(row == ROWS - 1, top, o)

    def prepare(which, raw, alpha, usable=None):
        targets[which], weights[which] = target_stack(raw, alpha, usable)

    fit_alpha, bridge_alpha = (LOG2E / (2.0 * v) for v in (DATA_VAR, BRIDGE_VAR))
    per = CHUNK // share
    halves = blocks // per

    def work(steps, after_step):
        top = score(*steps[0], 0)
        for i, step in enumerate(steps):
            next_top = score(*steps[i + 1], (i + 1) % 2) if i + 1 < len(steps) else None
            which, _, half = step
            o = weigh(which, i % 2, top)
            for j in range(per):
                at = half * per + j
                if which == 0:
                    at = at % 2 * pairs + at // 2
                parts[which, at] = o[:, j * share:(j + 1) * share]
            after_step(which, half)
            top = next_top

    load_x.wait()
    queries[0] = query_stack(x_ref[...])
    load_cells.wait()
    load_counts.wait()
    cell = c * cells_ref.shape[1] + lax.broadcasted_iota(jnp.int32, (1, cells_ref.shape[1]), 1)
    prepare(0, cells_ref[...], fit_alpha, cell < counts[t])
    work([(0, 0, half) for half in range(halves)], lambda which, half: None)
    sends = {}
    to_twin = remote(
        parts.at[0, pl.ds((1 - side) * pairs, pairs)], twin_sums,
        twin_sem.at[0], twin_sem.at[1], twin,
    )

    def merge(pieces):
        top = functools.reduce(jnp.maximum, [q[ROWS - 1:] for q in pieces])
        total = functools.reduce(jnp.add, [q * jnp.exp2(q[ROWS - 1:] - top) for q in pieces])
        return top, total

    def share_fit():
        to_twin.wait_recv()
        for j in range(pairs):
            top, total = merge([parts[0, side * pairs + j], twin_sums[j]])
            row = lax.broadcasted_iota(jnp.int32, total.shape, 0)
            pair_sums[j] = jnp.where(row == ROWS - 1, top, total)
        for k in range(1, pairs):
            sends[0, k] = remote(
                pair_sums.at[lax.rem(x + k, pairs)], got.at[0, k],
                part_send.at[0, k], part_recv.at[0, k], pair_to[k],
            )

    own = x_ref[:, mine]
    queries[1, :, (blocks - 1) * share:] = query_stack(own)

    def ready(which, half):
        if half == 0:
            i = which - 1
            pl.when(comes[i])(blocks_in[i].wait_recv)

            @pl.when(jnp.logical_not(comes[i]))
            def _():
                near[i] = jnp.zeros(near.shape[1:], f32)

            prepare(which, near[i], bridge_alpha)
        if which == 1:
            for i in range(half * per, min((half + 1) * per, blocks - 1)):
                slices_in[i].wait_recv()
                queries[1, :, i * share:(i + 1) * share] = query_stack(slices[i])

    def hand_back(which, half):
        if (which, half) == (2, 0):
            share_fit()
        for i in range(half * per, (half + 1) * per):
            if order[i]:
                sends[which, i] = remote(
                    parts.at[which, i], got.at[which, i],
                    part_send.at[which, i], part_recv.at[which, i], row_to[blocks - order[i]],
                    False,
                )

        @pl.when(comes[which - 1])
        def _():
            for i in range(half * per, (half + 1) * per):
                if order[i]:
                    sends[which, i].start()

    work([(which, 1, half) for half in range(halves) for which in (1, 2)], hand_back)

    def mean(which, home, alpha):
        pieces = [home] + [got[which, i] for kind, i in sends if kind == which]
        _, total = merge(pieces)
        return total[:30] / (total[30:31] * (2.0 * alpha))

    def settle(which, wait):
        for (kind, _), send in sends.items():
            if kind == which:
                wait(send)

    def settle_all(wait):
        settle(0, wait)
        for i in (0, 1):
            pl.when(comes[i])(functools.partial(settle, 1 + i, wait))

    settle_all(lambda send: send.wait_recv())
    fit_mean = mean(0, pair_sums[x], fit_alpha)
    prior_mean = mean(1, parts[1, blocks - 1], bridge_alpha)
    later_mean = mean(2, parts[2, blocks - 1], bridge_alpha)
    gradient = (own - fit_mean) / DATA_VAR
    gradient = gradient + jnp.where(has_prior, (own - prior_mean) / BRIDGE_VAR, 0.0)
    gradient = gradient + jnp.where(has_later, (own - later_mean) / BRIDGE_VAR, 0.0)
    load_noise.wait()
    g_out[:, 0, :] = gradient
    moved_out[:, 0, :] = (
        own + math.sqrt(2.0 * LANGEVIN_STRIDE * NOISE_LEVEL) * noise_ref[...]
    )
    settle_all(lambda send: send.wait_send())
    for go, copy in zip(goes, blocks_in):
        pl.when(go)(copy.wait_send)
    for copy in slices_in + [to_twin]:
        copy.wait_send()


def shards(sizes, particles, cell_points, cell_counts, brownian):
    _, dims, block = particles.shape
    cells = cell_points.shape[2]
    share = brownian.shape[2]
    _, blocks, peers = sizes
    assert blocks * share == block == cells and peers == blocks
    any_spec = pl.BlockSpec(memory_space=pl.ANY)
    dma = pltpu.SemaphoreType.DMA
    gradient, moved = pl.pallas_call(
        functools.partial(kernel, sizes),
        out_shape=[jax.ShapeDtypeStruct((dims, 1, share), f32)] * 2,
        in_specs=[any_spec] * 4,
        out_specs=[pl.BlockSpec(memory_space=pltpu.VMEM)] * 2,
        scratch_shapes=[
            pltpu.SMEM(cell_counts.shape, jnp.int32),
            pltpu.VMEM((dims, block), f32),
            pltpu.VMEM((dims, cells), f32),
            pltpu.VMEM((dims, share), f32),
            pltpu.VMEM((2, dims, block), f32),
            pltpu.VMEM((blocks, dims, share), f32),
            pltpu.VMEM((2, 6 * ROWS, block), bf16),
            pltpu.VMEM((3, block, 6 * ROWS), bf16),
            pltpu.VMEM((3, 2 * ROWS, block), bf16),
            pltpu.VMEM((2, block, CHUNK), f32),
            pltpu.VMEM((3, blocks, ROWS, share), f32),
            pltpu.VMEM((3, blocks, ROWS, share), f32),
            pltpu.VMEM((peers // 2, ROWS, share), f32),
            pltpu.VMEM((peers // 2, ROWS, share), f32),
            dma((4,)), dma((2,)), dma((2,)), dma((blocks,)), dma((blocks,)),
            dma((3, blocks)), dma((3, blocks)), dma((2,)),
        ],
        compiler_params=pltpu.CompilerParams(
            collective_id=0, has_side_effects=True, vmem_limit_bytes=2**26 - 64 * 2**10
        ),
        name="langevin",
    )(cell_counts, *(a.transpose(1, 0, 2) for a in (particles, cell_points, brownian)))
    gradient, moved = (a.transpose(1, 0, 2) for a in (gradient, moved))
    return -gradient, moved - LANGEVIN_STRIDE * gradient


def solution(mesh):
    in_specs = (
        P("tm", None, "particle"),
        P("tm", None, "cell"),
        P(),
        P("tm", None, ("particle", "cell")),
    )
    out_specs = (P("tm", None, ("particle", "cell")), P("tm", None, ("particle", "cell")))
    sizes = tuple(mesh.shape[a] for a in ("tm", "particle", "cell"))
    return jax.shard_map(
        functools.partial(shards, sizes),
        mesh=mesh, in_specs=in_specs, out_specs=out_specs, check_vma=False,
    )
```

```python
import functools
import math

import jax
import jax.numpy as jnp
from jax import lax
from jax.experimental import pallas as pl
from jax.experimental.pallas import tpu as pltpu
from jax.sharding import PartitionSpec as P

DATA_VAR = 2.0
BRIDGE_VAR = 1.5
LANGEVIN_STRIDE = 0.05
NOISE_LEVEL = 1.0
MASKED_SCORE = -1e30
LOG2E = math.log2(math.e)
MESH = pl.DeviceIdType.MESH
bf16, f32 = jnp.bfloat16, jnp.float32
ROWS = 32
CHUNK = 256


def split3(x):
    high = x.astype(bf16)
    rest = x - high.astype(f32)
    low = rest.astype(bf16)
    return high, low, (rest - low.astype(f32)).astype(bf16)


def query_stack(q):
    count = q.shape[1]
    ext = jnp.concatenate([q, jnp.ones((1, count), f32), jnp.zeros((1, count), f32)], 0)
    h, l, ll = split3(ext)
    return jnp.concatenate([h, h, l, l, h, ll], 0)


def target_stack(t, alpha, usable=None):
    count = t.shape[1]
    bias = -alpha * jnp.sum(t * t, 0, keepdims=True)
    if usable is not None:
        bias = jnp.where(usable, bias, MASKED_SCORE)
    ext = jnp.concatenate([t * (2.0 * alpha), bias, jnp.zeros((1, count), f32)], 0)
    h, l, ll = split3(ext)
    stack = jnp.concatenate([h, l, h, l, ll, h], 0)
    row = lax.broadcasted_iota(jnp.int32, ext.shape, 0)
    wh = jnp.where(row == 30, 1.0, h.astype(f32)).astype(bf16)
    wl = jnp.where(row == 30, 0.0, l.astype(f32)).astype(bf16)
    return stack.T, jnp.concatenate([wh, wl], 0)


def kernel(
    sizes,
    counts_hbm, x_hbm, cells_hbm, noise_hbm,
    g_out, moved_out,
    counts, x_ref, cells_ref, noise_ref, near, slices, queries, targets, weights, scores, parts, got, twin_sums, pair_sums,
    in_sem, near_send, near_recv, slice_send, slice_recv, part_send, part_recv, twin_sem,
):
    times, blocks, peers = sizes
    t, p, c = (lax.axis_index(a) for a in ("tm", "particle", "cell"))
    share = noise_ref.shape[1]
    order = sorted(range(blocks), key=lambda k: -min(k, blocks - k))
    mine = pl.ds(pl.multiple_of(c * share, share), share)

    def local(src, dst, sem):
        copy = pltpu.make_async_copy(src, dst, sem)
        copy.start()
        return copy

    def remote(src, dst, send, recv, device, start=True):
        copy = pltpu.make_async_remote_copy(
            src_ref=src, dst_ref=dst, send_sem=send, recv_sem=recv,
            device_id=device, device_id_type=MESH,
        )
        if start:
            copy.start()
        return copy

    after, before = lax.rem(t + 1, times), lax.rem(t + times - 1, times)
    times_near = [(after, p, c), (before, p, c)]
    has_prior, has_later = t > 0, t < times - 1
    goes, comes = (has_later, has_prior), (has_prior, has_later)
    row_to = {k: (t, lax.rem(p + k, blocks), c) for k in range(1, blocks)}
    pairs = peers // 2
    x, side = lax.div(c, 2), lax.rem(c, 2)
    twin = (t, p, 2 * x + 1 - side)
    pair_to = {k: (t, p, 2 * lax.rem(x + k, pairs) + side) for k in range(1, pairs)}
    greeted = [row_to[k] for k in order if k] + [twin] + list(pair_to.values())
    barrier = pltpu.get_barrier_semaphore()

    def greet(device):
        pl.semaphore_signal(barrier, inc=1, device_id=device, device_id_type=MESH)

    for device in greeted[:2]:
        greet(device)
    for go, device in zip(goes, times_near):
        pl.when(go)(functools.partial(greet, device))
    for device in greeted[2:]:
        greet(device)
    load_x = local(x_hbm.at[:, 0, :], x_ref, in_sem.at[0])
    load_cells = local(cells_hbm.at[:, 0, :], cells_ref, in_sem.at[1])
    load_noise = local(noise_hbm.at[:, 0, :], noise_ref, in_sem.at[2])
    load_counts = local(counts_hbm, counts, in_sem.at[3])
    pl.semaphore_wait(
        barrier, len(greeted) + has_prior.astype(jnp.int32) + has_later.astype(jnp.int32)
    )

    blocks_in = [
        remote(x_hbm.at[:, 0, :], near.at[i], near_send.at[i], near_recv.at[i], device, False)
        for i, device in enumerate(times_near)
    ]
    pl.when(goes[0])(blocks_in[0].start)
    slices_in = [
        remote(x_hbm.at[:, 0, mine], slices.at[i], slice_send.at[i], slice_recv.at[i], row_to[k])
        for i, k in enumerate(order) if k
    ]

    pl.when(goes[1])(blocks_in[1].start)

    def score(which, queries_at, half, slot):
        if which:
            ready(which, half)
        s = jnp.dot(
            targets[which], queries[queries_at, :, half * CHUNK:(half + 1) * CHUNK],
            preferred_element_type=f32,
        )
        scores[slot] = s
        return jnp.max(s, 0, keepdims=True)

    def weigh(which, slot, top):
        e = jnp.exp2(scores[slot] - top)
        eh = e.astype(bf16)
        el = (e - eh.astype(f32)).astype(bf16)
        o = jnp.dot(weights[which], eh, preferred_element_type=f32)
        o = o[:ROWS] + o[ROWS:]
        o = o + jnp.dot(weights[which, :ROWS], el, preferred_element_type=f32)
        row = lax.broadcasted_iota(jnp.int32, o.shape, 0)
        return jnp.where(row == ROWS - 1, top, o)

    def prepare(which, raw, alpha, usable=None):
        targets[which], weights[which] = target_stack(raw, alpha, usable)

    fit_alpha, bridge_alpha = (LOG2E / (2.0 * v) for v in (DATA_VAR, BRIDGE_VAR))
    per = CHUNK // share
    halves = blocks // per

    def work(steps, after_step):
        top = score(*steps[0], 0)
        for i, step in enumerate(steps):
            next_top = score(*steps[i + 1], (i + 1) % 2) if i + 1 < len(steps) else None
            which, _, half = step
            o = weigh(which, i % 2, top)
            for j in range(per):
                at = half * per + j
                if which == 0:
                    at = at % 2 * pairs + at // 2
                parts[which, at] = o[:, j * share:(j + 1) * share]
            after_step(which, half)
            top = next_top

    load_x.wait()
    queries[0] = query_stack(x_ref[...])
    load_cells.wait()
    load_counts.wait()
    cell = c * cells_ref.shape[1] + lax.broadcasted_iota(jnp.int32, (1, cells_ref.shape[1]), 1)
    prepare(0, cells_ref[...], fit_alpha, cell < counts[t])
    work([(0, 0, half) for half in range(halves)], lambda which, half: None)
    sends = {}
    to_twin = remote(
        parts.at[0, pl.ds((1 - side) * pairs, pairs)], twin_sums,
        twin_sem.at[0], twin_sem.at[1], twin,
    )

    def merge(pieces):
        top = functools.reduce(jnp.maximum, [q[ROWS - 1:] for q in pieces])
        total = functools.reduce(jnp.add, [q * jnp.exp2(q[ROWS - 1:] - top) for q in pieces])
        return top, total

    def share_fit():
        to_twin.wait_recv()
        for j in range(pairs):
            top, total = merge([parts[0, side * pairs + j], twin_sums[j]])
            row = lax.broadcasted_iota(jnp.int32, total.shape, 0)
            pair_sums[j] = jnp.where(row == ROWS - 1, top, total)
        for k in range(1, pairs):
            sends[0, k] = remote(
                pair_sums.at[lax.rem(x + k, pairs)], got.at[0, k],
                part_send.at[0, k], part_recv.at[0, k], pair_to[k],
            )

    own = x_ref[:, mine]
    queries[1, :, (blocks - 1) * share:] = query_stack(own)

    def ready(which, half):
        if half == 0:
            i = which - 1
            pl.when(comes[i])(blocks_in[i].wait_recv)

            @pl.when(jnp.logical_not(comes[i]))
            def _():
                near[i] = jnp.zeros(near.shape[1:], f32)

            prepare(which, near[i], bridge_alpha)
        if which == 1:
            for i in range(half * per, min((half + 1) * per, blocks - 1)):
                slices_in[i].wait_recv()
                queries[1, :, i * share:(i + 1) * share] = query_stack(slices[i])

    def hand_back(which, half):
        if (which, half) == (2, 0):
            share_fit()
        for i in range(half * per, (half + 1) * per):
            if order[i]:
                sends[which, i] = remote(
                    parts.at[which, i], got.at[which, i],
                    part_send.at[which, i], part_recv.at[which, i], row_to[blocks - order[i]],
                    False,
                )

        @pl.when(comes[which - 1])
        def _():
            for i in range(half * per, (half + 1) * per):
                if order[i]:
                    sends[which, i].start()

    work([(which, 1, half) for which in (1, 2) for half in range(halves)], hand_back)

    def mean(which, home, alpha):
        pieces = [home] + [got[which, i] for kind, i in sends if kind == which]
        _, total = merge(pieces)
        return total[:30] / (total[30:31] * (2.0 * alpha))

    def settle(which, wait):
        for (kind, _), send in sends.items():
            if kind == which:
                wait(send)

    def settle_all(wait):
        settle(0, wait)
        for i in (0, 1):
            pl.when(comes[i])(functools.partial(settle, 1 + i, wait))

    arrive = lambda send: send.wait_recv()
    settle(0, arrive)
    fit_mean = mean(0, pair_sums[x], fit_alpha)
    pl.when(comes[0])(functools.partial(settle, 1, arrive))
    prior_mean = mean(1, parts[1, blocks - 1], bridge_alpha)
    pl.when(comes[1])(functools.partial(settle, 2, arrive))
    later_mean = mean(2, parts[2, blocks - 1], bridge_alpha)
    gradient = (own - fit_mean) / DATA_VAR
    gradient = gradient + jnp.where(has_prior, (own - prior_mean) / BRIDGE_VAR, 0.0)
    gradient = gradient + jnp.where(has_later, (own - later_mean) / BRIDGE_VAR, 0.0)
    load_noise.wait()
    g_out[:, 0, :] = gradient
    moved_out[:, 0, :] = (
        own + math.sqrt(2.0 * LANGEVIN_STRIDE * NOISE_LEVEL) * noise_ref[...]
    )
    settle_all(lambda send: send.wait_send())
    for go, copy in zip(goes, blocks_in):
        pl.when(go)(copy.wait_send)
    for copy in slices_in + [to_twin]:
        copy.wait_send()


def shards(sizes, particles, cell_points, cell_counts, brownian):
    _, dims, block = particles.shape
    cells = cell_points.shape[2]
    share = brownian.shape[2]
    _, blocks, peers = sizes
    assert blocks * share == block == cells and peers == blocks
    any_spec = pl.BlockSpec(memory_space=pl.ANY)
    dma = pltpu.SemaphoreType.DMA
    gradient, moved = pl.pallas_call(
        functools.partial(kernel, sizes),
        out_shape=[jax.ShapeDtypeStruct((dims, 1, share), f32)] * 2,
        in_specs=[any_spec] * 4,
        out_specs=[pl.BlockSpec(memory_space=pltpu.VMEM)] * 2,
        scratch_shapes=[
            pltpu.SMEM(cell_counts.shape, jnp.int32),
            pltpu.VMEM((dims, block), f32),
            pltpu.VMEM((dims, cells), f32),
            pltpu.VMEM((dims, share), f32),
            pltpu.VMEM((2, dims, block), f32),
            pltpu.VMEM((blocks, dims, share), f32),
            pltpu.VMEM((2, 6 * ROWS, block), bf16),
            pltpu.VMEM((3, block, 6 * ROWS), bf16),
            pltpu.VMEM((3, 2 * ROWS, block), bf16),
            pltpu.VMEM((2, block, CHUNK), f32),
            pltpu.VMEM((3, blocks, ROWS, share), f32),
            pltpu.VMEM((3, blocks, ROWS, share), f32),
            pltpu.VMEM((peers // 2, ROWS, share), f32),
            pltpu.VMEM((peers // 2, ROWS, share), f32),
            dma((4,)), dma((2,)), dma((2,)), dma((blocks,)), dma((blocks,)),
            dma((3, blocks)), dma((3, blocks)), dma((2,)),
        ],
        compiler_params=pltpu.CompilerParams(
            collective_id=0, has_side_effects=True, vmem_limit_bytes=2**26 - 64 * 2**10
        ),
        name="langevin",
    )(cell_counts, *(a.transpose(1, 0, 2) for a in (particles, cell_points, brownian)))
    gradient, moved = (a.transpose(1, 0, 2) for a in (gradient, moved))
    return -gradient, moved - LANGEVIN_STRIDE * gradient


def solution(mesh):
    in_specs = (
        P("tm", None, "particle"),
        P("tm", None, "cell"),
        P(),
        P("tm", None, ("particle", "cell")),
    )
    out_specs = (P("tm", None, ("particle", "cell")), P("tm", None, ("particle", "cell")))
    sizes = tuple(mesh.shape[a] for a in ("tm", "particle", "cell"))
    return jax.shard_map(
        functools.partial(shards, sizes),
        mesh=mesh, in_specs=in_specs, out_specs=out_specs, check_vma=False,
    )
```

```python
import functools
import math

import jax
import jax.numpy as jnp
from jax import lax
from jax.experimental import pallas as pl
from jax.experimental.pallas import tpu as pltpu
from jax.sharding import PartitionSpec as P

DATA_VAR = 2.0
BRIDGE_VAR = 1.5
LANGEVIN_STRIDE = 0.05
NOISE_LEVEL = 1.0
MASKED_SCORE = -1e30
LOG2E = math.log2(math.e)
MESH = pl.DeviceIdType.MESH
bf16, f32 = jnp.bfloat16, jnp.float32
ROWS = 32
CHUNK = 256


def split3(x):
    high = x.astype(bf16)
    rest = x - high.astype(f32)
    low = rest.astype(bf16)
    return high, low, (rest - low.astype(f32)).astype(bf16)


def query_stack(q):
    count = q.shape[1]
    ext = jnp.concatenate([q, jnp.ones((1, count), f32), jnp.zeros((1, count), f32)], 0)
    h, l, ll = split3(ext)
    return jnp.concatenate([h, h, l, l, h, ll], 0)


def target_stack(t, alpha, usable=None):
    count = t.shape[1]
    bias = -alpha * jnp.sum(t * t, 0, keepdims=True)
    if usable is not None:
        bias = jnp.where(usable, bias, MASKED_SCORE)
    ext = jnp.concatenate([t * (2.0 * alpha), bias, jnp.zeros((1, count), f32)], 0)
    h, l, ll = split3(ext)
    stack = jnp.concatenate([h, l, h, l, ll, h], 0)
    row = lax.broadcasted_iota(jnp.int32, ext.shape, 0)
    wh = jnp.where(row == 30, 1.0, h.astype(f32)).astype(bf16)
    wl = jnp.where(row == 30, 0.0, l.astype(f32)).astype(bf16)
    return stack.T, jnp.concatenate([wh, wl], 0)


def kernel(
    sizes,
    counts_hbm, x_hbm, cells_hbm, noise_hbm,
    g_out, moved_out,
    counts, x_ref, cells_ref, noise_ref, near, slices, queries, targets, weights, scores, parts, got, side_sums, pair_sums,
    in_sem, near_send, near_recv, slice_send, slice_recv, part_send, part_recv, twin_sem,
):
    times, blocks, peers = sizes
    t, p, c = (lax.axis_index(a) for a in ("tm", "particle", "cell"))
    share = noise_ref.shape[1]
    order = sorted(range(blocks), key=lambda k: -min(k, blocks - k))
    mine = pl.ds(pl.multiple_of(c * share, share), share)

    def local(src, dst, sem):
        copy = pltpu.make_async_copy(src, dst, sem)
        copy.start()
        return copy

    def remote(src, dst, send, recv, device, start=True):
        copy = pltpu.make_async_remote_copy(
            src_ref=src, dst_ref=dst, send_sem=send, recv_sem=recv,
            device_id=device, device_id_type=MESH,
        )
        if start:
            copy.start()
        return copy

    after, before = lax.rem(t + 1, times), lax.rem(t + times - 1, times)
    times_near = [(after, p, c), (before, p, c)]
    has_prior, has_later = t > 0, t < times - 1
    goes, comes = (has_later, has_prior), (has_prior, has_later)
    row_to = {k: (t, lax.rem(p + k, blocks), c) for k in range(1, blocks)}
    pairs = peers // 2
    x, side = lax.div(c, 2), lax.rem(c, 2)
    twin = (t, p, 2 * x + 1 - side)
    pair_to = {k: (t, p, 2 * lax.rem(x + k, pairs) + side) for k in range(1, pairs)}
    greeted = [row_to[k] for k in order if k] + [twin] + list(pair_to.values())
    barrier = pltpu.get_barrier_semaphore()

    def greet(device):
        pl.semaphore_signal(barrier, inc=1, device_id=device, device_id_type=MESH)

    for device in greeted[:2]:
        greet(device)
    for go, device in zip(goes, times_near):
        pl.when(go)(functools.partial(greet, device))
    for device in greeted[2:]:
        greet(device)
    load_x = local(x_hbm.at[:, 0, :], x_ref, in_sem.at[0])
    load_cells = local(cells_hbm.at[:, 0, :], cells_ref, in_sem.at[1])
    load_noise = local(noise_hbm.at[:, 0, :], noise_ref, in_sem.at[2])
    load_counts = local(counts_hbm, counts, in_sem.at[3])
    pl.semaphore_wait(
        barrier, len(greeted) + has_prior.astype(jnp.int32) + has_later.astype(jnp.int32)
    )

    blocks_in = [
        remote(x_hbm.at[:, 0, :], near.at[i], near_send.at[i], near_recv.at[i], device, False)
        for i, device in enumerate(times_near)
    ]
    pl.when(goes[0])(blocks_in[0].start)
    slices_in = [
        remote(x_hbm.at[:, 0, mine], slices.at[i], slice_send.at[i], slice_recv.at[i], row_to[k])
        for i, k in enumerate(order) if k
    ]

    pl.when(goes[1])(blocks_in[1].start)

    def score(which, queries_at, half, slot):
        if which:
            ready(which, half)
        s = jnp.dot(
            targets[which], queries[queries_at, :, half * CHUNK:(half + 1) * CHUNK],
            preferred_element_type=f32,
        )
        scores[slot] = s
        return jnp.max(s, 0, keepdims=True)

    def weigh(which, slot, top):
        e = jnp.exp2(scores[slot] - top)
        eh = e.astype(bf16)
        el = (e - eh.astype(f32)).astype(bf16)
        o = jnp.dot(weights[which], eh, preferred_element_type=f32)
        o = o[:ROWS] + o[ROWS:]
        o = o + jnp.dot(weights[which, :ROWS], el, preferred_element_type=f32)
        row = lax.broadcasted_iota(jnp.int32, o.shape, 0)
        return jnp.where(row == ROWS - 1, top, o)

    def prepare(which, raw, alpha, usable=None):
        targets[which], weights[which] = target_stack(raw, alpha, usable)

    fit_alpha, bridge_alpha = (LOG2E / (2.0 * v) for v in (DATA_VAR, BRIDGE_VAR))
    per = CHUNK // share
    halves = blocks // per

    def work(steps, after_step):
        top = score(*steps[0], 0)
        for i, step in enumerate(steps):
            next_top = score(*steps[i + 1], (i + 1) % 2) if i + 1 < len(steps) else None
            which, _, half = step
            o = weigh(which, i % 2, top)
            for j in range(per):
                at = half * per + j
                parts[which, at] = o[:, j * share:(j + 1) * share]
            after_step(which, half)
            top = next_top

    load_x.wait()
    queries[0] = query_stack(x_ref[...])
    load_cells.wait()
    load_counts.wait()
    cell = c * cells_ref.shape[1] + lax.broadcasted_iota(jnp.int32, (1, cells_ref.shape[1]), 1)
    prepare(0, cells_ref[...], fit_alpha, cell < counts[t])
    work([(0, 0, half) for half in range(halves)], lambda which, half: None)
    sends = {}
    to_pairs = [
        remote(
            parts.at[0, pl.ds(2 * lax.rem(x + k, pairs), 2)], side_sums.at[k - 1],
            part_send.at[0, k], part_recv.at[0, k], pair_to[k],
        )
        for k in range(1, pairs)
    ]

    def merge(pieces):
        top = functools.reduce(jnp.maximum, [q[ROWS - 1:] for q in pieces])
        total = functools.reduce(jnp.add, [q * jnp.exp2(q[ROWS - 1:] - top) for q in pieces])
        return top, total

    def share_fit():
        for copy in to_pairs:
            copy.wait_recv()
        for j in range(2):
            top, total = merge([parts[0, 2 * x + j]] + [side_sums[k, j] for k in range(pairs - 1)])
            row = lax.broadcasted_iota(jnp.int32, total.shape, 0)
            pair_sums[j] = jnp.where(row == ROWS - 1, top, total)
        sends[0, 0] = remote(
            pair_sums.at[1 - side], got.at[0, 0], twin_sem.at[0], twin_sem.at[1], twin
        )

    own = x_ref[:, mine]
    queries[1, :, (blocks - 1) * share:] = query_stack(own)

    def ready(which, half):
        if half == 0:
            i = which - 1
            pl.when(comes[i])(blocks_in[i].wait_recv)

            @pl.when(jnp.logical_not(comes[i]))
            def _():
                near[i] = jnp.zeros(near.shape[1:], f32)

            prepare(which, near[i], bridge_alpha)
        if which == 1:
            for i in range(half * per, min((half + 1) * per, blocks - 1)):
                slices_in[i].wait_recv()
                queries[1, :, i * share:(i + 1) * share] = query_stack(slices[i])

    def hand_back(which, half):
        if (which, half) == (2, 0):
            share_fit()
        for i in range(half * per, (half + 1) * per):
            if order[i]:
                sends[which, i] = remote(
                    parts.at[which, i], got.at[which, i],
                    part_send.at[which, i], part_recv.at[which, i], row_to[blocks - order[i]],
                    False,
                )

        @pl.when(comes[which - 1])
        def _():
            for i in range(half * per, (half + 1) * per):
                if order[i]:
                    sends[which, i].start()

    work([(which, 1, half) for which in (1, 2) for half in range(halves)], hand_back)

    def mean(which, home, alpha):
        pieces = [home] + [got[which, i] for kind, i in sends if kind == which]
        _, total = merge(pieces)
        return total[:30] / (total[30:31] * (2.0 * alpha))

    def settle(which, wait):
        for (kind, _), send in sends.items():
            if kind == which:
                wait(send)

    def settle_all(wait):
        settle(0, wait)
        for i in (0, 1):
            pl.when(comes[i])(functools.partial(settle, 1 + i, wait))

    arrive = lambda send: send.wait_recv()
    settle(0, arrive)
    fit_mean = mean(0, pair_sums[side], fit_alpha)
    pl.when(comes[0])(functools.partial(settle, 1, arrive))
    prior_mean = mean(1, parts[1, blocks - 1], bridge_alpha)
    pl.when(comes[1])(functools.partial(settle, 2, arrive))
    later_mean = mean(2, parts[2, blocks - 1], bridge_alpha)
    gradient = (own - fit_mean) / DATA_VAR
    gradient = gradient + jnp.where(has_prior, (own - prior_mean) / BRIDGE_VAR, 0.0)
    gradient = gradient + jnp.where(has_later, (own - later_mean) / BRIDGE_VAR, 0.0)
    load_noise.wait()
    g_out[:, 0, :] = gradient
    moved_out[:, 0, :] = (
        own + math.sqrt(2.0 * LANGEVIN_STRIDE * NOISE_LEVEL) * noise_ref[...]
    )
    settle_all(lambda send: send.wait_send())
    for go, copy in zip(goes, blocks_in):
        pl.when(go)(copy.wait_send)
    for copy in slices_in + to_pairs:
        copy.wait_send()


def shards(sizes, particles, cell_points, cell_counts, brownian):
    _, dims, block = particles.shape
    cells = cell_points.shape[2]
    share = brownian.shape[2]
    _, blocks, peers = sizes
    assert blocks * share == block == cells and peers == blocks
    any_spec = pl.BlockSpec(memory_space=pl.ANY)
    dma = pltpu.SemaphoreType.DMA
    gradient, moved = pl.pallas_call(
        functools.partial(kernel, sizes),
        out_shape=[jax.ShapeDtypeStruct((dims, 1, share), f32)] * 2,
        in_specs=[any_spec] * 4,
        out_specs=[pl.BlockSpec(memory_space=pltpu.VMEM)] * 2,
        scratch_shapes=[
            pltpu.SMEM(cell_counts.shape, jnp.int32),
            pltpu.VMEM((dims, block), f32),
            pltpu.VMEM((dims, cells), f32),
            pltpu.VMEM((dims, share), f32),
            pltpu.VMEM((2, dims, block), f32),
            pltpu.VMEM((blocks, dims, share), f32),
            pltpu.VMEM((2, 6 * ROWS, block), bf16),
            pltpu.VMEM((3, block, 6 * ROWS), bf16),
            pltpu.VMEM((3, 2 * ROWS, block), bf16),
            pltpu.VMEM((2, block, CHUNK), f32),
            pltpu.VMEM((3, blocks, ROWS, share), f32),
            pltpu.VMEM((3, blocks, ROWS, share), f32),
            pltpu.VMEM((peers // 2 - 1, 2, ROWS, share), f32),
            pltpu.VMEM((2, ROWS, share), f32),
            dma((4,)), dma((2,)), dma((2,)), dma((blocks,)), dma((blocks,)),
            dma((3, blocks)), dma((3, blocks)), dma((2,)),
        ],
        compiler_params=pltpu.CompilerParams(
            collective_id=0, has_side_effects=True, vmem_limit_bytes=2**26 - 64 * 2**10
        ),
        name="langevin",
    )(cell_counts, *(a.transpose(1, 0, 2) for a in (particles, cell_points, brownian)))
    gradient, moved = (a.transpose(1, 0, 2) for a in (gradient, moved))
    return -gradient, moved - LANGEVIN_STRIDE * gradient


def solution(mesh):
    in_specs = (
        P("tm", None, "particle"),
        P("tm", None, "cell"),
        P(),
        P("tm", None, ("particle", "cell")),
    )
    out_specs = (P("tm", None, ("particle", "cell")), P("tm", None, ("particle", "cell")))
    sizes = tuple(mesh.shape[a] for a in ("tm", "particle", "cell"))
    return jax.shard_map(
        functools.partial(shards, sizes),
        mesh=mesh, in_specs=in_specs, out_specs=out_specs, check_vma=False,
    )
```

```python
import functools
import math

import jax
import jax.numpy as jnp
from jax import lax
from jax.experimental import pallas as pl
from jax.experimental.pallas import tpu as pltpu
from jax.sharding import PartitionSpec as P

DATA_VAR = 2.0
BRIDGE_VAR = 1.5
LANGEVIN_STRIDE = 0.05
NOISE_LEVEL = 1.0
MASKED_SCORE = -1e30
LOG2E = math.log2(math.e)
MESH = pl.DeviceIdType.MESH
bf16, f32 = jnp.bfloat16, jnp.float32
ROWS = 32
CHUNK = 256


def split3(x):
    high = x.astype(bf16)
    rest = x - high.astype(f32)
    low = rest.astype(bf16)
    return high, low, (rest - low.astype(f32)).astype(bf16)


def query_stack(q):
    count = q.shape[1]
    ext = jnp.concatenate([q, jnp.ones((1, count), f32), jnp.zeros((1, count), f32)], 0)
    h, l, ll = split3(ext)
    return jnp.concatenate([h, h, l, l, h, ll], 0)


def target_stack(t, alpha, usable=None):
    count = t.shape[1]
    bias = -alpha * jnp.sum(t * t, 0, keepdims=True)
    if usable is not None:
        bias = jnp.where(usable, bias, MASKED_SCORE)
    ext = jnp.concatenate([t * (2.0 * alpha), bias, jnp.zeros((1, count), f32)], 0)
    h, l, ll = split3(ext)
    stack = jnp.concatenate([h, l, h, l, ll, h], 0)
    row = lax.broadcasted_iota(jnp.int32, ext.shape, 0)
    wh = jnp.where(row == 30, 1.0, h.astype(f32)).astype(bf16)
    wl = jnp.where(row == 30, 0.0, l.astype(f32)).astype(bf16)
    return stack.T, jnp.concatenate([wh, wl], 0)


def kernel(
    sizes,
    counts_hbm, x_hbm, cells_hbm, noise_hbm,
    g_out, moved_out,
    counts, x_ref, cells_ref, noise_ref, near, slices, queries, targets, weights, scores, parts, got, side_sums, pair_sums,
    in_sem, near_send, near_recv, slice_send, slice_recv, part_send, part_recv, twin_sem,
):
    times, blocks, peers = sizes
    t, p, c = (lax.axis_index(a) for a in ("tm", "particle", "cell"))
    share = noise_ref.shape[1]
    order = sorted(range(blocks), key=lambda k: -min(k, blocks - k))
    mine = pl.ds(pl.multiple_of(c * share, share), share)

    def local(src, dst, sem):
        copy = pltpu.make_async_copy(src, dst, sem)
        copy.start()
        return copy

    def remote(src, dst, send, recv, device, start=True):
        copy = pltpu.make_async_remote_copy(
            src_ref=src, dst_ref=dst, send_sem=send, recv_sem=recv,
            device_id=device, device_id_type=MESH,
        )
        if start:
            copy.start()
        return copy

    after, before = lax.rem(t + 1, times), lax.rem(t + times - 1, times)
    times_near = [(after, p, c), (before, p, c)]
    has_prior, has_later = t > 0, t < times - 1
    goes, comes = (has_later, has_prior), (has_prior, has_later)
    row_to = {k: (t, lax.rem(p + k, blocks), c) for k in range(1, blocks)}
    pairs = peers // 2
    x, side = lax.div(c, 2), lax.rem(c, 2)
    twin = (t, p, 2 * x + 1 - side)
    pair_to = {k: (t, p, 2 * lax.rem(x + k, pairs) + side) for k in range(1, pairs)}
    greeted = [row_to[k] for k in order if k] + [twin] + list(pair_to.values())
    barrier = pltpu.get_barrier_semaphore()

    def greet(device):
        pl.semaphore_signal(barrier, inc=1, device_id=device, device_id_type=MESH)

    for device in greeted[:2]:
        greet(device)
    for go, device in zip(goes, times_near):
        pl.when(go)(functools.partial(greet, device))
    for device in greeted[2:]:
        greet(device)
    load_x = local(x_hbm.at[:, 0, :], x_ref, in_sem.at[0])
    load_cells = local(cells_hbm.at[:, 0, :], cells_ref, in_sem.at[1])
    load_noise = local(noise_hbm.at[:, 0, :], noise_ref, in_sem.at[2])
    load_counts = local(counts_hbm, counts, in_sem.at[3])
    pl.semaphore_wait(
        barrier, len(greeted) + has_prior.astype(jnp.int32) + has_later.astype(jnp.int32)
    )

    blocks_in = [
        remote(x_hbm.at[:, 0, :], near.at[i], near_send.at[i], near_recv.at[i], device, False)
        for i, device in enumerate(times_near)
    ]
    pl.when(goes[0])(blocks_in[0].start)
    slices_in = [
        remote(x_hbm.at[:, 0, mine], slices.at[i], slice_send.at[i], slice_recv.at[i], row_to[k])
        for i, k in enumerate(order) if k
    ]

    pl.when(goes[1])(blocks_in[1].start)

    def score(which, queries_at, half, slot):
        if which == 1:
            ready(1, half)
            if half == halves - 1:
                ready(2, 0)
        s = jnp.dot(
            targets[which], queries[queries_at, :, half * CHUNK:(half + 1) * CHUNK],
            preferred_element_type=f32,
        )
        scores[slot] = s
        return jnp.max(s, 0, keepdims=True)

    def weigh(which, slot, top):
        e = jnp.exp2(scores[slot] - top)
        eh = e.astype(bf16)
        el = (e - eh.astype(f32)).astype(bf16)
        o = jnp.dot(weights[which], eh, preferred_element_type=f32)
        o = o[:ROWS] + o[ROWS:]
        o = o + jnp.dot(weights[which, :ROWS], el, preferred_element_type=f32)
        row = lax.broadcasted_iota(jnp.int32, o.shape, 0)
        return jnp.where(row == ROWS - 1, top, o)

    def prepare(which, raw, alpha, usable=None):
        targets[which], weights[which] = target_stack(raw, alpha, usable)

    fit_alpha, bridge_alpha = (LOG2E / (2.0 * v) for v in (DATA_VAR, BRIDGE_VAR))
    per = CHUNK // share
    halves = blocks // per

    def work(steps, after_step):
        top = score(*steps[0], 0)
        for i, step in enumerate(steps):
            next_top = score(*steps[i + 1], (i + 1) % 2) if i + 1 < len(steps) else None
            which, _, half = step
            o = weigh(which, i % 2, top)
            for j in range(per):
                at = half * per + j
                parts[which, at] = o[:, j * share:(j + 1) * share]
            after_step(which, half)
            top = next_top

    load_x.wait()
    queries[0] = query_stack(x_ref[...])
    load_cells.wait()
    load_counts.wait()
    cell = c * cells_ref.shape[1] + lax.broadcasted_iota(jnp.int32, (1, cells_ref.shape[1]), 1)
    prepare(0, cells_ref[...], fit_alpha, cell < counts[t])
    work([(0, 0, half) for half in range(halves)], lambda which, half: None)
    sends = {}
    to_pairs = [
        remote(
            parts.at[0, pl.ds(2 * lax.rem(x + k, pairs), 2)], side_sums.at[k - 1],
            part_send.at[0, k], part_recv.at[0, k], pair_to[k],
        )
        for k in range(1, pairs)
    ]

    def merge(pieces):
        top = functools.reduce(jnp.maximum, [q[ROWS - 1:] for q in pieces])
        total = functools.reduce(jnp.add, [q * jnp.exp2(q[ROWS - 1:] - top) for q in pieces])
        return top, total

    def share_fit():
        for copy in to_pairs:
            copy.wait_recv()
        for j in range(2):
            top, total = merge([parts[0, 2 * x + j]] + [side_sums[k, j] for k in range(pairs - 1)])
            row = lax.broadcasted_iota(jnp.int32, total.shape, 0)
            pair_sums[j] = jnp.where(row == ROWS - 1, top, total)
        sends[0, 0] = remote(
            pair_sums.at[1 - side], got.at[0, 0], twin_sem.at[0], twin_sem.at[1], twin
        )

    own = x_ref[:, mine]
    queries[1, :, (blocks - 1) * share:] = query_stack(own)

    def ready(which, half):
        if half == 0:
            i = which - 1
            pl.when(comes[i])(blocks_in[i].wait_recv)

            @pl.when(jnp.logical_not(comes[i]))
            def _():
                near[i] = jnp.zeros(near.shape[1:], f32)

            prepare(which, near[i], bridge_alpha)
        if which == 1:
            for i in range(half * per, min((half + 1) * per, blocks - 1)):
                slices_in[i].wait_recv()
                queries[1, :, i * share:(i + 1) * share] = query_stack(slices[i])

    def hand_back(which, half):
        if (which, half) == (2, 0):
            share_fit()
        for i in range(half * per, (half + 1) * per):
            if order[i]:
                sends[which, i] = remote(
                    parts.at[which, i], got.at[which, i],
                    part_send.at[which, i], part_recv.at[which, i], row_to[blocks - order[i]],
                    False,
                )

        @pl.when(comes[which - 1])
        def _():
            for i in range(half * per, (half + 1) * per):
                if order[i]:
                    sends[which, i].start()

    work([(which, 1, half) for which in (1, 2) for half in range(halves)], hand_back)

    def mean(which, home, alpha):
        pieces = [home] + [got[which, i] for kind, i in sends if kind == which]
        _, total = merge(pieces)
        return total[:30] / (total[30:31] * (2.0 * alpha))

    def settle(which, wait):
        for (kind, _), send in sends.items():
            if kind == which:
                wait(send)

    def settle_all(wait):
        settle(0, wait)
        for i in (0, 1):
            pl.when(comes[i])(functools.partial(settle, 1 + i, wait))

    arrive = lambda send: send.wait_recv()
    settle(0, arrive)
    fit_mean = mean(0, pair_sums[side], fit_alpha)
    pl.when(comes[0])(functools.partial(settle, 1, arrive))
    prior_mean = mean(1, parts[1, blocks - 1], bridge_alpha)
    pl.when(comes[1])(functools.partial(settle, 2, arrive))
    later_mean = mean(2, parts[2, blocks - 1], bridge_alpha)
    gradient = (own - fit_mean) / DATA_VAR
    gradient = gradient + jnp.where(has_prior, (own - prior_mean) / BRIDGE_VAR, 0.0)
    gradient = gradient + jnp.where(has_later, (own - later_mean) / BRIDGE_VAR, 0.0)
    load_noise.wait()
    g_out[:, 0, :] = gradient
    moved_out[:, 0, :] = (
        own + math.sqrt(2.0 * LANGEVIN_STRIDE * NOISE_LEVEL) * noise_ref[...]
    )
    settle_all(lambda send: send.wait_send())
    for go, copy in zip(goes, blocks_in):
        pl.when(go)(copy.wait_send)
    for copy in slices_in + to_pairs:
        copy.wait_send()


def shards(sizes, particles, cell_points, cell_counts, brownian):
    _, dims, block = particles.shape
    cells = cell_points.shape[2]
    share = brownian.shape[2]
    _, blocks, peers = sizes
    assert blocks * share == block == cells and peers == blocks
    any_spec = pl.BlockSpec(memory_space=pl.ANY)
    dma = pltpu.SemaphoreType.DMA
    gradient, moved = pl.pallas_call(
        functools.partial(kernel, sizes),
        out_shape=[jax.ShapeDtypeStruct((dims, 1, share), f32)] * 2,
        in_specs=[any_spec] * 4,
        out_specs=[pl.BlockSpec(memory_space=pltpu.VMEM)] * 2,
        scratch_shapes=[
            pltpu.SMEM(cell_counts.shape, jnp.int32),
            pltpu.VMEM((dims, block), f32),
            pltpu.VMEM((dims, cells), f32),
            pltpu.VMEM((dims, share), f32),
            pltpu.VMEM((2, dims, block), f32),
            pltpu.VMEM((blocks, dims, share), f32),
            pltpu.VMEM((2, 6 * ROWS, block), bf16),
            pltpu.VMEM((3, block, 6 * ROWS), bf16),
            pltpu.VMEM((3, 2 * ROWS, block), bf16),
            pltpu.VMEM((2, block, CHUNK), f32),
            pltpu.VMEM((3, blocks, ROWS, share), f32),
            pltpu.VMEM((3, blocks, ROWS, share), f32),
            pltpu.VMEM((peers // 2 - 1, 2, ROWS, share), f32),
            pltpu.VMEM((2, ROWS, share), f32),
            dma((4,)), dma((2,)), dma((2,)), dma((blocks,)), dma((blocks,)),
            dma((3, blocks)), dma((3, blocks)), dma((2,)),
        ],
        compiler_params=pltpu.CompilerParams(
            collective_id=0, has_side_effects=True, vmem_limit_bytes=2**26 - 64 * 2**10
        ),
        name="langevin",
    )(cell_counts, *(a.transpose(1, 0, 2) for a in (particles, cell_points, brownian)))
    gradient, moved = (a.transpose(1, 0, 2) for a in (gradient, moved))
    return -gradient, moved - LANGEVIN_STRIDE * gradient


def solution(mesh):
    in_specs = (
        P("tm", None, "particle"),
        P("tm", None, "cell"),
        P(),
        P("tm", None, ("particle", "cell")),
    )
    out_specs = (P("tm", None, ("particle", "cell")), P("tm", None, ("particle", "cell")))
    sizes = tuple(mesh.shape[a] for a in ("tm", "particle", "cell"))
    return jax.shard_map(
        functools.partial(shards, sizes),
        mesh=mesh, in_specs=in_specs, out_specs=out_specs, check_vma=False,
    )
```
